32 devices in a mesh: row: 4 (over y, x), col: 8 (over z, core).
Axes of the slice: x: 2, y: 2, z: 4, core: 2. Of those that a mesh axis runs over, the one named last changes fastest.
Arguments:
- rhs: float32 [1536, 3072], P('row', 'col'), may hold values from -6 to 6
- a_pair: float32 [1536, 6144], P('row', 'col'), may hold values from -0.15625 to 0.15625
- b_pair: float32 [3072, 3072], P('row', 'col'), may hold values from -0.15625 to 0.15625
- u_cay: float32 [1536, 384], P('row'), may hold values from -1 to 1, as said below
- v_cay: float32 [384, 3072], P(None, 'col'), may hold values from -1 to 1, as said below
Outputs:
- solved: float32 [1536, 3072], P('row', 'col')
The draws below stay inside these ranges and needn't reach their ends.
Inputs may be any that keep to these rules, and one draw needn't show every extreme that they name: `u_cay`: each 384 x 384 block of rows has spectral radius below 1. `v_cay`: each 384 x 384 block of columns has spectral radius below 1.
All inputs are finite; a program needn't handle non-finite values.
Results may differ from the reference program's by a relative error of at most 0.0001.
Values sent between devices are 32-bit elements; how exact they have to be, the bound alone decides.
A program may use at most 64 MiB of HBM per device.

```python
import math
import jax
import jax.numpy as jnp
from jax import lax

NB = 384
ITERS = 3
N = 1536
M = 3072
FRONT = 3


def cayley_blocks(key, block_count):
    key_noise, key_size, key_signs = jax.random.split(key, 3)
    normal_draw = jax.random.normal(key_noise, (block_count, NB, NB), jnp.float32)
    symmetric = (normal_draw + jnp.swapaxes(normal_draw, 1, 2)) * (0.1 / math.sqrt(2.0 * NB))
    magnitude = jnp.exp(jax.random.uniform(key_size, (block_count, NB), jnp.float32, math.log(0.05), math.log(0.75)))
    signs = jnp.where(jax.random.bernoulli(key_signs, 0.5, (block_count, NB)), 1.0, -1.0)
    diagonal = jnp.eye(NB, dtype=jnp.float32)[None, :, :] * (signs * magnitude)[:, :, None]
    return symmetric + diagonal


def draw_u_cay(key, part):
    return cayley_blocks(jax.random.fold_in(key, 11), N // NB).reshape(N, NB)


def draw_v_cay(key, part):
    stacked = cayley_blocks(jax.random.fold_in(key, 12), M // NB)
    return stacked.transpose(1, 0, 2).reshape(NB, M)


def block_scale(key, dims, cuts, low, high):
    def one(position, parts):
        heights = jax.random.uniform(jax.random.fold_in(jax.random.fold_in(key, 6), position), (parts,), jnp.float32, low / len(cuts), high / len(cuts))
        return jnp.repeat(jnp.exp(heights), dims[position] // parts).reshape((-1,) + (1,) * (len(dims) - position - 1))

    loudness = one(*cuts[0])
    for cut in cuts[1:]:
        loudness = loudness * one(*cut)
    return loudness


def bell_draw(rng, extent, spread, most, shards=(), kind=jnp.bfloat16):
    values = spread * jax.random.normal(rng, extent, jnp.float32)
    if shards:
        values = values * block_scale(rng, extent, shards, -0.22, 0.18)
    return jnp.clip(values, -most, most).astype(kind)


def setup_inputs(seed: int = 0) -> dict:
    splits = jax.random.split(jax.random.key(seed), 6)
    rhs = bell_draw(splits[0], (N, M), 1.0, 6.0, ((0, 4), (1, 8)), jnp.float32)
    a_pair = bell_draw(splits[1], (N, 2 * M), (4 * NB) ** -0.5, 0.15625, ((0, 4), (1, 8)), jnp.float32)
    b_pair = bell_draw(splits[2], (2 * N, M), (4 * NB) ** -0.5, 0.15625, ((0, 4), (1, 8)), jnp.float32)
    u_cay = draw_u_cay(jax.random.fold_in(splits[5], 71), 0)
    v_cay = draw_v_cay(jax.random.fold_in(splits[5], 71), 0)
    return {"rhs": rhs, "a_pair": a_pair, "b_pair": b_pair, "u_cay": u_cay, "v_cay": v_cay}


precise = lax.Precision.HIGHEST


def product(left_side, right_side):
    return jnp.dot(left_side, right_side, precision=precise, preferred_element_type=jnp.float32)


def powers(matrix):
    result = [matrix]
    for step_index in range(ITERS - 1):
        result.append(product(result[-1], result[-1]))
    return result


def doubling(u_powers, v_powers, right_side):
    scaled = right_side + product(u_powers[0], right_side)
    iterate = 0.5 * (scaled + product(scaled, v_powers[0]))
    for u_power, v_power in zip(u_powers, v_powers):
        iterate = iterate + product(u_power, product(iterate, v_power))
    return iterate


def solve_block(u_block, v_block, right_side):
    return doubling(powers(u_block), powers(v_block), right_side)


def reference(rhs, a_pair, b_pair, u_cay, v_cay):
    row_count = N // NB
    col_count = M // NB
    blocks = rhs.reshape(row_count, NB, col_count, NB).transpose(0, 2, 1, 3)
    a_blocks = a_pair.reshape(row_count, NB, col_count, 2, NB).transpose(0, 2, 3, 1, 4)
    b_blocks = b_pair.reshape(row_count, 2, NB, col_count, NB).transpose(0, 3, 1, 2, 4)
    u_blocks = u_cay.reshape(row_count, NB, NB)
    v_blocks = v_cay.reshape(NB, col_count, NB).transpose(1, 0, 2)
    row_ids = jnp.arange(row_count, dtype=jnp.int32)
    col_ids = jnp.arange(col_count, dtype=jnp.int32)
    first_cols = (FRONT - row_ids).astype(jnp.int32)
    second_cols = (FRONT + 1 - row_ids).astype(jnp.int32)
    first_x = jax.vmap(solve_block)(u_blocks, v_blocks[first_cols], blocks[row_ids, first_cols])
    above = jnp.concatenate([jnp.zeros((1, NB, NB), first_x.dtype), first_x[:-1]], axis=0)
    a_near = a_blocks[row_ids, second_cols, 0]
    b_near = b_blocks[row_ids, second_cols, 0]
    right_side = blocks[row_ids, second_cols] - (jax.vmap(product)(a_near, above) + jax.vmap(product)(first_x, b_near))
    second_x = jax.vmap(solve_block)(u_blocks, v_blocks[second_cols], right_side)
    first_rows = (FRONT - col_ids).astype(jnp.int32)
    second_rows = (FRONT + 1 - col_ids).astype(jnp.int32)
    first_valid = (first_rows >= 0) & (first_rows < row_count)
    second_valid = (second_rows >= 0) & (second_rows < row_count)
    col_first = jnp.where(first_valid[:, None, None], first_x[jnp.clip(first_rows, 0, row_count - 1)], 0.0)
    col_second = jnp.where(second_valid[:, None, None], second_x[jnp.clip(second_rows, 0, row_count - 1)], 0.0)
    col_stack = jnp.stack([col_first, col_second])
    row_stack = jnp.stack([first_x, second_x])
    a_term = jnp.einsum('ijfab,fjbc->ijac', a_blocks, col_stack, precision=precise)
    b_term = jnp.einsum('fiab,ijfbc->ijac', row_stack, b_blocks, precision=precise)
    updated = blocks - (a_term + b_term)
    block_sum = row_ids[:, None] + col_ids[None, :]
    result = jnp.where((block_sum >= FRONT + 2)[:, :, None, None], updated, blocks)
    result = result.at[row_ids, first_cols].set(first_x)
    result = result.at[row_ids, second_cols].set(second_x)
    return result.transpose(0, 2, 1, 3).reshape(N, M)
```

```python
import functools

import jax
import jax.numpy as jnp
from jax import lax
from jax.experimental import pallas as pl
from jax.experimental.pallas import tpu as pltpu
from jax.sharding import PartitionSpec as P

ITERS = 3
CHUNKS = 6
LEFT_1, ABOVE_1, LEFT_2, ABOVE_2 = range(4)
MESH = pl.DeviceIdType.MESH


def parts(x):
    high = x.astype(jnp.bfloat16)
    low = (x - high.astype(jnp.float32)).astype(jnp.bfloat16)
    return high, low


def as_left(x):
    high, low = parts(x)
    return jnp.concatenate([high, high, low], axis=1)


def as_right(x):
    high, low = parts(x)
    return jnp.concatenate([high, low, high], axis=0)


def product(left_side, right_side):
    return jnp.dot(left_side, right_side, preferred_element_type=jnp.float32)


def kernel(rows, cols, rhs_ref, a_ref, b_ref, u_ref, v_ref, out_ref, held, lefts, rights,
           total, send_sem, recv_sem):
    i, j = lax.axis_index("row"), lax.axis_index("col")
    nb = rhs_ref.shape[0]
    size = nb // CHUNKS
    front = rows - 1
    s = i + j
    on_first, on_second, on_trail = s == front, s == front + 1, s >= front + 2
    place = {"row": (i, rows), "col": (j, cols)}

    barrier = pltpu.get_barrier_semaphore()
    count = jnp.int32(0)
    for axis, (k, n) in place.items():
        for by in (-2, -1, 1, 2):
            there = (k + by >= 0) & (k + by < n)
            count = count + there.astype(jnp.int32)

            @pl.when(there)
            def _():
                pl.semaphore_signal(barrier, inc=1, device_id={axis: k + by}, device_id_type=MESH)

    def flow_axis(flow):
        return "col" if flow in (LEFT_1, LEFT_2) else "row"

    def each_send(flow, holds, is_source, source, c, act):
        axis = flow_axis(flow)
        k, n = place[axis]
        even = lax.rem(k, 2) == 0
        span = pl.ds(pl.multiple_of(c * size, size), size)
        for slot, by in ((1, 2), (0, 1)):
            goes = holds & (k + by < n) & (even if by == 2 else (even | is_source))

            @pl.when(goes)
            def _():
                act(pltpu.make_async_remote_copy(
                    src_ref=source.at[span], dst_ref=held.at[flow, span],
                    send_sem=send_sem.at[flow, slot, c], recv_sem=recv_sem.at[flow, c],
                    device_id={axis: k + by}, device_id_type=MESH))

    def receive(flow, c):
        span = pl.ds(pl.multiple_of(c * size, size), size)
        pltpu.make_async_remote_copy(
            src_ref=held.at[flow, span], dst_ref=held.at[flow, span],
            send_sem=send_sem.at[flow, 0, c], recv_sem=recv_sem.at[flow, c],
            device_id={"row": i}, device_id_type=MESH).wait_recv()

    start = lambda copy: copy.start()
    wait_send = lambda copy: copy.wait_send()
    no = jnp.bool_(False)
    yes = jnp.bool_(True)

    def relay(flows):
        def step(c, carry):
            for flow, valid in flows:
                @pl.when(valid)
                def _():
                    receive(flow, c)
                    each_send(flow, yes, no, held.at[flow], c, start)
            return carry
        lax.fori_loop(0, CHUNKS, step, 0)

    above_1 = j <= front
    above_2 = j <= front + 1

    @pl.when(on_first | on_second)
    def _():
        for source, sides, make in ((u_ref, lefts, as_left), (v_ref, rights, as_right)):
            power = source[...]
            sides[0] = make(power)
            for step in range(1, ITERS):
                if make is as_left:
                    power = product(sides[step - 1], as_right(power))
                else:
                    power = product(as_left(power), sides[step - 1])
                sides[step] = make(power)
        total[...] = rhs_ref[...]

    @pl.when(jnp.logical_not(on_first | on_second))
    def _():
        out_ref[...] = rhs_ref[...]

    @pl.when(on_second)
    def _():
        lefts[ITERS] = as_left(a_ref[:, :nb])
        rights[ITERS] = as_right(b_ref[:nb, :])

    @pl.when(on_trail)
    def _():
        for step in range(2):
            lefts[step] = as_left(a_ref[:, step * nb:(step + 1) * nb])
            rights[step] = as_right(b_ref[step * nb:(step + 1) * nb, :])

    pl.semaphore_wait(barrier, count)

    @pl.when(s > front)
    def _():
        relay(((LEFT_1, yes), (ABOVE_1, above_1)))

    @pl.when(on_second)
    def _():
        total[...] -= product(as_left(held[LEFT_1]), rights[ITERS])

        @pl.when(above_1)
        def _():
            total[...] -= product(lefts[ITERS], as_right(held[ABOVE_1]))

    @pl.when(on_first | on_second)
    def _():
        block = total[...]
        scaled = block + product(lefts[0], as_right(block))
        iterate = 0.5 * (scaled + product(as_left(scaled), rights[0]))
        for step in range(ITERS):
            middle = product(as_left(iterate), rights[step])
            iterate = iterate + product(lefts[step], as_right(middle))
        out_ref[...] = iterate

        def step(c, carry):
            each_send(LEFT_1, on_first, yes, out_ref, c, start)
            each_send(ABOVE_1, on_first, yes, out_ref, c, start)
            each_send(LEFT_2, on_second, yes, out_ref, c, start)
            each_send(ABOVE_2, on_second, yes, out_ref, c, start)
            return carry
        lax.fori_loop(0, CHUNKS, step, 0)

    @pl.when(on_trail)
    def _():
        total[...] = product(as_left(held[LEFT_1]), rights[0])

        @pl.when(above_1)
        def _():
            total[...] += product(lefts[0], as_right(held[ABOVE_1]))

        relay(((LEFT_2, yes), (ABOVE_2, above_2)))

        total[...] += product(as_left(held[LEFT_2]), rights[1])

        @pl.when(above_2)
        def _():
            total[...] += product(lefts[1], as_right(held[ABOVE_2]))

        out_ref[...] = rhs_ref[...] - total[...]

    def finish(c, carry):
        each_send(LEFT_1, s >= front, on_first, held.at[LEFT_1], c, wait_send)
        each_send(ABOVE_1, (s >= front) & above_1, on_first, held.at[ABOVE_1], c, wait_send)
        each_send(LEFT_2, s >= front + 1, on_second, held.at[LEFT_2], c, wait_send)
        each_send(ABOVE_2, (s >= front + 1) & above_2, on_second, held.at[ABOVE_2], c, wait_send)
        return carry
    lax.fori_loop(0, CHUNKS, finish, 0)


def body(rows, cols, rhs, a_pair, b_pair, u_cay, v_cay):
    nb = rhs.shape[0]
    return pl.pallas_call(
        functools.partial(kernel, rows, cols),
        out_shape=jax.ShapeDtypeStruct(rhs.shape, jnp.float32),
        in_specs=[pl.BlockSpec(memory_space=pltpu.VMEM)] * 5,
        out_specs=pl.BlockSpec(memory_space=pltpu.VMEM),
        scratch_shapes=[
            pltpu.VMEM((4, nb, nb), jnp.float32),
            pltpu.VMEM((ITERS + 1, nb, 3 * nb), jnp.bfloat16),
            pltpu.VMEM((ITERS + 1, 3 * nb, nb), jnp.bfloat16),
            pltpu.VMEM((nb, nb), jnp.float32),
            pltpu.SemaphoreType.DMA((4, 2, CHUNKS)),
            pltpu.SemaphoreType.DMA((4, CHUNKS)),
        ],
        compiler_params=pltpu.CompilerParams(
            collective_id=0, has_side_effects=True, vmem_limit_bytes=40 * 2**20
        ),
    )(rhs, a_pair, b_pair, u_cay, v_cay)


def solution(mesh):
    placed = (P("row", "col"), P("row", "col"), P("row", "col"), P("row", None), P(None, "col"))
    return jax.shard_map(
        functools.partial(body, mesh.shape["row"], mesh.shape["col"]),
        mesh=mesh, in_specs=placed, out_specs=P("row", "col"), check_vma=False,
    )
```

```python
import functools

import jax
import jax.numpy as jnp
from jax import lax
from jax.experimental import pallas as pl
from jax.experimental.pallas import tpu as pltpu
from jax.sharding import PartitionSpec as P

ITERS = 3
CHUNKS = 6
PIECES = 3
LEFT_1, ABOVE_1, LEFT_2, ABOVE_2 = range(4)
MESH = pl.DeviceIdType.MESH


def parts(x):
    high = x.astype(jnp.bfloat16)
    low = (x - high.astype(jnp.float32)).astype(jnp.bfloat16)
    return high, low


def as_left(x):
    high, low = parts(x)
    return jnp.concatenate([high, high, low], axis=1)


def as_right(x):
    high, low = parts(x)
    return jnp.concatenate([high, low, high], axis=0)


def product(left_side, right_side):
    return jnp.dot(left_side, right_side, preferred_element_type=jnp.float32)


def kernel(rows, cols, rhs_in, a_in, b_in, u_in, v_in, out_ref, rhs_ref, a_ref, b_ref, u_ref,
           v_ref, held, lefts, rights, total, send_sem, recv_sem, load_sem):
    i, j = lax.axis_index("row"), lax.axis_index("col")
    nb = rhs_ref.shape[0]
    size = nb // CHUNKS
    front = rows - 1
    s = i + j
    on_first, on_second, on_trail = s == front, s == front + 1, s >= front + 2
    place = {"row": (i, rows), "col": (j, cols)}
    on_front = on_first | on_second

    def load(which, act):
        origin, target = (
            (u_in, u_ref), (v_in, v_ref), (rhs_in, rhs_ref), (a_in, a_ref), (b_in, b_ref)
        )[which]
        depth = origin.shape[0] // PIECES
        for piece in range(PIECES):
            span = pl.ds(piece * depth, depth)
            act(pltpu.make_async_copy(
                origin.at[span], target.at[span], load_sem.at[which, piece]))

    start = lambda copy: copy.start()
    wait = lambda copy: copy.wait()

    @pl.when(on_front)
    def _():
        load(0, start)
        load(1, start)

    load(2, start)

    @pl.when(s > front)
    def _():
        load(3, start)
        load(4, start)

    barrier = pltpu.get_barrier_semaphore()
    count = jnp.int32(0)
    for axis, (k, n) in place.items():
        for by in (-2, -1, 1, 2):
            there = (k + by >= 0) & (k + by < n)
            count = count + there.astype(jnp.int32)

            @pl.when(there)
            def _():
                pl.semaphore_signal(barrier, inc=1, device_id={axis: k + by}, device_id_type=MESH)

    def flow_axis(flow):
        return "col" if flow in (LEFT_1, LEFT_2) else "row"

    def forwards(flow):
        k, n = place[flow_axis(flow)]
        return (lax.rem(k, 2) == 0) & (k + 1 < n)

    def each_send(flow, holds, is_source, source, c, act, hops=(2, 1)):
        axis = flow_axis(flow)
        k, n = place[axis]
        even = lax.rem(k, 2) == 0
        span = pl.ds(pl.multiple_of(c * size, size), size)
        for by in hops:
            slot = by - 1
            goes = holds & (k + by < n) & (even if by == 2 else (even | is_source))

            @pl.when(goes)
            def _():
                act(pltpu.make_async_remote_copy(
                    src_ref=source.at[span], dst_ref=held.at[flow, span],
                    send_sem=send_sem.at[flow, slot, c], recv_sem=recv_sem.at[flow, c],
                    device_id={axis: k + by}, device_id_type=MESH))

    def receive(flow, c):
        span = pl.ds(pl.multiple_of(c * size, size), size)
        pltpu.make_async_remote_copy(
            src_ref=held.at[flow, span], dst_ref=held.at[flow, span],
            send_sem=send_sem.at[flow, 0, c], recv_sem=recv_sem.at[flow, c],
            device_id={"row": i}, device_id_type=MESH).wait_recv()

    wait_send = lambda copy: copy.wait_send()
    no = jnp.bool_(False)
    yes = jnp.bool_(True)

    def relay(flows):
        def step(c, carry):
            for flow, valid in flows:
                @pl.when(valid & forwards(flow))
                def _():
                    receive(flow, c)
                    each_send(flow, yes, no, held.at[flow], c, start)
            return carry
        lax.fori_loop(0, CHUNKS, step, 0)

    def collect(flow, valid):
        @pl.when(valid & jnp.logical_not(forwards(flow)))
        def _():
            def step(c, carry):
                receive(flow, c)
                return carry
            lax.fori_loop(0, CHUNKS, step, 0)

    above_1 = j <= front
    above_2 = j <= front + 1

    @pl.when(on_front)
    def _():
        for which, source, sides, make in (
            (0, u_ref, lefts, as_left), (1, v_ref, rights, as_right)
        ):
            load(which, wait)
            power = source[...]
            sides[0] = make(power)
            for step in range(1, ITERS):
                if make is as_left:
                    power = product(sides[step - 1], as_right(power))
                else:
                    power = product(as_left(power), sides[step - 1])
                sides[step] = make(power)

    load(2, wait)

    @pl.when(on_front)
    def _():
        total[...] = rhs_ref[...]

    @pl.when(s < front)
    def _():
        out_ref[...] = rhs_ref[...]

    @pl.when(s > front)
    def _():
        load(3, wait)
        load(4, wait)

    @pl.when(on_second)
    def _():
        lefts[ITERS] = as_left(a_ref[:, :nb])
        rights[ITERS] = as_right(b_ref[:nb, :])

    @pl.when(on_trail)
    def _():
        for step in range(2):
            lefts[step] = as_left(a_ref[:, step * nb:(step + 1) * nb])
            rights[step] = as_right(b_ref[step * nb:(step + 1) * nb, :])

    pl.semaphore_wait(barrier, count)

    @pl.when(s > front)
    def _():
        relay(((LEFT_1, yes), (ABOVE_1, above_1)))
        collect(LEFT_1, yes)
        collect(ABOVE_1, above_1)

    @pl.when(on_second)
    def _():
        total[...] -= product(as_left(held[LEFT_1]), rights[ITERS])

        @pl.when(above_1)
        def _():
            total[...] -= product(lefts[ITERS], as_right(held[ABOVE_1]))

    @pl.when(on_front)
    def _():
        block = total[...]
        scaled = block + product(lefts[0], as_right(block))
        iterate = 0.5 * (scaled + product(as_left(scaled), rights[0]))
        for step in range(ITERS):
            middle = product(as_left(iterate), rights[step])
            iterate = iterate + product(lefts[step], as_right(middle))
        out_ref[...] = iterate

        def step(c, carry):
            each_send(LEFT_1, on_first, yes, out_ref, c, start)
            each_send(ABOVE_1, on_first, yes, out_ref, c, start, (1,))
            each_send(LEFT_2, on_second, yes, out_ref, c, start)
            each_send(ABOVE_2, on_second, yes, out_ref, c, start)
            return carry
        lax.fori_loop(0, CHUNKS, step, 0)

        @pl.when(on_first)
        def _():
            def urgent(c, carry):
                each_send(ABOVE_1, yes, yes, out_ref, c, wait_send, (1,))
                return carry
            lax.fori_loop(0, CHUNKS, urgent, 0)

            def later(c, carry):
                each_send(ABOVE_1, yes, yes, out_ref, c, start, (2,))
                return carry
            lax.fori_loop(0, CHUNKS, later, 0)

    @pl.when(on_trail)
    def _():
        total[...] = product(as_left(held[LEFT_1]), rights[0])

        @pl.when(above_1)
        def _():
            total[...] += product(lefts[0], as_right(held[ABOVE_1]))

        relay(((LEFT_2, yes), (ABOVE_2, above_2)))
        collect(LEFT_2, yes)

        total[...] += product(as_left(held[LEFT_2]), rights[1])
        collect(ABOVE_2, above_2)

        @pl.when(above_2)
        def _():
            total[...] += product(lefts[1], as_right(held[ABOVE_2]))

        out_ref[...] = rhs_ref[...] - total[...]

    def finish(c, carry):
        each_send(LEFT_1, s >= front, on_first, held.at[LEFT_1], c, wait_send)
        each_send(ABOVE_1, (s > front) & above_1, no, held.at[ABOVE_1], c, wait_send)
        each_send(ABOVE_1, on_first, yes, held.at[ABOVE_1], c, wait_send, (2,))
        each_send(LEFT_2, s >= front + 1, on_second, held.at[LEFT_2], c, wait_send)
        each_send(ABOVE_2, (s >= front + 1) & above_2, on_second, held.at[ABOVE_2], c, wait_send)
        return carry
    lax.fori_loop(0, CHUNKS, finish, 0)


def body(rows, cols, rhs, a_pair, b_pair, u_cay, v_cay):
    nb = rhs.shape[0]
    return pl.pallas_call(
        functools.partial(kernel, rows, cols),
        out_shape=jax.ShapeDtypeStruct(rhs.shape, jnp.float32),
        in_specs=[pl.BlockSpec(memory_space=pltpu.HBM)] * 5,
        out_specs=pl.BlockSpec(memory_space=pltpu.VMEM),
        scratch_shapes=[
            pltpu.VMEM(rhs.shape, jnp.float32),
            pltpu.VMEM(a_pair.shape, jnp.float32),
            pltpu.VMEM(b_pair.shape, jnp.float32),
            pltpu.VMEM(u_cay.shape, jnp.float32),
            pltpu.VMEM(v_cay.shape, jnp.float32),
            pltpu.VMEM((4, nb, nb), jnp.float32),
            pltpu.VMEM((ITERS + 1, nb, 3 * nb), jnp.bfloat16),
            pltpu.VMEM((ITERS + 1, 3 * nb, nb), jnp.bfloat16),
            pltpu.VMEM((nb, nb), jnp.float32),
            pltpu.SemaphoreType.DMA((4, 2, CHUNKS)),
            pltpu.SemaphoreType.DMA((4, CHUNKS)),
            pltpu.SemaphoreType.DMA((5, PIECES)),
        ],
        compiler_params=pltpu.CompilerParams(
            collective_id=0, has_side_effects=True, vmem_limit_bytes=62 * 2**20
        ),
    )(rhs, a_pair, b_pair, u_cay, v_cay)


def solution(mesh):
    placed = (P("row", "col"), P("row", "col"), P("row", "col"), P("row", None), P(None, "col"))
    return jax.shard_map(
        functools.partial(body, mesh.shape["row"], mesh.shape["col"]),
        mesh=mesh, in_specs=placed, out_specs=P("row", "col"), check_vma=False,
    )
```

```python
import functools

import jax
import jax.numpy as jnp
from jax import lax
from jax.experimental import pallas as pl
from jax.experimental.pallas import tpu as pltpu
from jax.sharding import PartitionSpec as P

ITERS = 3
CHUNKS = 6
PIECES = 3
SLABS = 3
LEFT_1, ABOVE_1, LEFT_2, ABOVE_2 = range(4)
MESH = pl.DeviceIdType.MESH


def parts(x):
    high = x.astype(jnp.bfloat16)
    low = (x - high.astype(jnp.float32)).astype(jnp.bfloat16)
    return high, low


def as_left(x):
    high, low = parts(x)
    return jnp.concatenate([high, high, low], axis=1)


def as_right(x):
    high, low = parts(x)
    return jnp.concatenate([high, low, high], axis=0)


def product(left_side, right_side):
    return jnp.dot(left_side, right_side, preferred_element_type=jnp.float32)


def kernel(rows, cols, rhs_in, a_in, b_in, u_in, v_in, out_ref, rhs_ref, a_ref, b_ref, u_ref,
           v_ref, held, lefts, rights, total, send_sem, recv_sem, load_sem):
    i, j = lax.axis_index("row"), lax.axis_index("col")
    nb = rhs_ref.shape[0]
    size = nb // CHUNKS
    front = rows - 1
    s = i + j
    on_first, on_second, on_trail = s == front, s == front + 1, s >= front + 2
    place = {"row": (i, rows), "col": (j, cols)}
    on_front = on_first | on_second

    def load(which, act):
        origin, target = (
            (u_in, u_ref), (v_in, v_ref), (rhs_in, rhs_ref), (a_in, a_ref), (b_in, b_ref)
        )[which]
        depth = origin.shape[0] // PIECES
        for piece in range(PIECES):
            span = pl.ds(piece * depth, depth)
            act(pltpu.make_async_copy(
                origin.at[span], target.at[span], load_sem.at[which, piece]))

    start = lambda copy: copy.start()
    wait = lambda copy: copy.wait()

    @pl.when(on_front)
    def _():
        load(0, start)
        load(1, start)

    load(2, start)

    @pl.when(s > front)
    def _():
        load(3, start)
        load(4, start)

    barrier = pltpu.get_barrier_semaphore()
    count = jnp.int32(0)
    for axis, (k, n) in place.items():
        for by in (-2, -1, 1, 2):
            there = (k + by >= 0) & (k + by < n)
            count = count + there.astype(jnp.int32)

            @pl.when(there)
            def _():
                pl.semaphore_signal(barrier, inc=1, device_id={axis: k + by}, device_id_type=MESH)

    def flow_axis(flow):
        return "col" if flow in (LEFT_1, LEFT_2) else "row"

    def hops(flow):
        axis = flow_axis(flow)
        k, n = place[axis]
        even = lax.rem(k, 2) == 0
        source = front + (flow in (LEFT_2, ABOVE_2)) - (i if axis == "col" else j)
        if axis == "col":
            return (1, (k + 1 < n) & (even | (k == source))), (2, (k + 2 < n) & even)
        odd_source = (source & 1) == 1
        return (
            (1, (k + 1 < n) & even & (k != source + 1)),
            (2, (k + 2 < n) & (even | (k == source))),
            (-1, odd_source & (k == source + 2)),
        )

    def forwards(flow):
        return functools.reduce(jnp.logical_or, [goes for _, goes in hops(flow)])

    def each_send(flow, holds, source, c, act):
        axis = flow_axis(flow)
        k, _ = place[axis]
        span = pl.ds(pl.multiple_of(c * size, size), size)
        for slot, (by, goes) in enumerate(hops(flow)):
            @pl.when(holds & goes)
            def _():
                act(pltpu.make_async_remote_copy(
                    src_ref=source.at[span], dst_ref=held.at[flow, span],
                    send_sem=send_sem.at[flow, slot, c], recv_sem=recv_sem.at[flow, c],
                    device_id={axis: k + by}, device_id_type=MESH))

    def receive(flow, c):
        span = pl.ds(pl.multiple_of(c * size, size), size)
        pltpu.make_async_remote_copy(
            src_ref=held.at[flow, span], dst_ref=held.at[flow, span],
            send_sem=send_sem.at[flow, 0, c], recv_sem=recv_sem.at[flow, c],
            device_id={"row": i}, device_id_type=MESH).wait_recv()

    wait_send = lambda copy: copy.wait_send()
    yes = jnp.bool_(True)

    def relay(flows):
        def step(c, carry):
            for flow, valid in flows:
                @pl.when(valid & forwards(flow))
                def _():
                    receive(flow, c)
                    each_send(flow, yes, held.at[flow], c, start)
            return carry
        lax.fori_loop(0, CHUNKS, step, 0)

    def collect(flow, valid):
        @pl.when(valid & jnp.logical_not(forwards(flow)))
        def _():
            def step(c, carry):
                receive(flow, c)
                return carry
            lax.fori_loop(0, CHUNKS, step, 0)

    above_1 = j <= front
    above_2 = j <= front + 1

    @pl.when(on_front)
    def _():
        for which, source, sides, make in (
            (0, u_ref, lefts, as_left), (1, v_ref, rights, as_right)
        ):
            load(which, wait)
            power = source[...]
            sides[0] = make(power)
            for step in range(1, ITERS):
                if make is as_left:
                    power = product(sides[step - 1], as_right(power))
                else:
                    power = product(as_left(power), sides[step - 1])
                sides[step] = make(power)

    load(2, wait)

    @pl.when(on_front)
    def _():
        total[...] = rhs_ref[...]

    @pl.when(s < front)
    def _():
        out_ref[...] = rhs_ref[...]

    @pl.when(s > front)
    def _():
        load(3, wait)
        load(4, wait)

    @pl.when(on_second)
    def _():
        lefts[ITERS] = as_left(a_ref[:, :nb])
        rights[ITERS] = as_right(b_ref[:nb, :])

    @pl.when(on_trail)
    def _():
        for step in range(2):
            lefts[step] = as_left(a_ref[:, step * nb:(step + 1) * nb])
            rights[step] = as_right(b_ref[step * nb:(step + 1) * nb, :])

    pl.semaphore_wait(barrier, count)

    @pl.when(s > front)
    def _():
        relay(((ABOVE_1, above_1), (LEFT_1, yes)))
        collect(LEFT_1, yes)
        collect(ABOVE_1, above_1)

    @pl.when(on_second)
    def _():
        total[...] -= product(as_left(held[LEFT_1]), rights[ITERS])

        @pl.when(above_1)
        def _():
            total[...] -= product(lefts[ITERS], as_right(held[ABOVE_1]))

    @pl.when(on_front)
    def _():
        block = total[...]
        scaled = block + product(lefts[0], as_right(block))
        iterate = 0.5 * (scaled + product(as_left(scaled), rights[0]))
        for step in range(ITERS - 1):
            middle = product(as_left(iterate), rights[step])
            iterate = iterate + product(lefts[step], as_right(middle))
        total[...] = iterate
        rights[ITERS] = as_right(product(as_left(iterate), rights[ITERS - 1]))

        def send(c, carry):
            each_send(ABOVE_1, on_first, out_ref, c, start)
            each_send(LEFT_1, on_first, out_ref, c, start)
            each_send(LEFT_2, on_second, out_ref, c, start)
            each_send(ABOVE_2, on_second, out_ref, c, start)
            return carry

        depth = nb // SLABS
        for slab in range(SLABS):
            span = pl.ds(slab * depth, depth)
            out_ref[span] = total[span] + product(lefts[ITERS - 1, span], rights[ITERS])
            each = CHUNKS // SLABS
            lax.fori_loop(slab * each, (slab + 1) * each, send, 0)

    @pl.when(on_trail)
    def _():
        total[...] = product(as_left(held[LEFT_1]), rights[0])

        @pl.when(above_1)
        def _():
            total[...] += product(lefts[0], as_right(held[ABOVE_1]))

        relay(((LEFT_2, yes), (ABOVE_2, above_2)))
        collect(LEFT_2, yes)

        total[...] += product(as_left(held[LEFT_2]), rights[1])
        collect(ABOVE_2, above_2)

        @pl.when(above_2)
        def _():
            total[...] += product(lefts[1], as_right(held[ABOVE_2]))

        out_ref[...] = rhs_ref[...] - total[...]

    def finish(c, carry):
        each_send(LEFT_1, s >= front, held.at[LEFT_1], c, wait_send)
        each_send(ABOVE_1, (s >= front) & above_1, held.at[ABOVE_1], c, wait_send)
        each_send(LEFT_2, s >= front + 1, held.at[LEFT_2], c, wait_send)
        each_send(ABOVE_2, (s >= front + 1) & above_2, held.at[ABOVE_2], c, wait_send)
        return carry
    lax.fori_loop(0, CHUNKS, finish, 0)


def body(rows, cols, rhs, a_pair, b_pair, u_cay, v_cay):
    nb = rhs.shape[0]
    return pl.pallas_call(
        functools.partial(kernel, rows, cols),
        out_shape=jax.ShapeDtypeStruct(rhs.shape, jnp.float32),
        in_specs=[pl.BlockSpec(memory_space=pltpu.HBM)] * 5,
        out_specs=pl.BlockSpec(memory_space=pltpu.VMEM),
        scratch_shapes=[
            pltpu.VMEM(rhs.shape, jnp.float32),
            pltpu.VMEM(a_pair.shape, jnp.float32),
            pltpu.VMEM(b_pair.shape, jnp.float32),
            pltpu.VMEM(u_cay.shape, jnp.float32),
            pltpu.VMEM(v_cay.shape, jnp.float32),
            pltpu.VMEM((4, nb, nb), jnp.float32),
            pltpu.VMEM((ITERS + 1, nb, 3 * nb), jnp.bfloat16),
            pltpu.VMEM((ITERS + 1, 3 * nb, nb), jnp.bfloat16),
            pltpu.VMEM((nb, nb), jnp.float32),
            pltpu.SemaphoreType.DMA((4, 3, CHUNKS)),
            pltpu.SemaphoreType.DMA((4, CHUNKS)),
            pltpu.SemaphoreType.DMA((5, PIECES)),
        ],
        compiler_params=pltpu.CompilerParams(
            collective_id=0, has_side_effects=True, vmem_limit_bytes=62 * 2**20
        ),
    )(rhs, a_pair, b_pair, u_cay, v_cay)


def solution(mesh):
    placed = (P("row", "col"), P("row", "col"), P("row", "col"), P("row", None), P(None, "col"))
    return jax.shard_map(
        functools.partial(body, mesh.shape["row"], mesh.shape["col"]),
        mesh=mesh, in_specs=placed, out_specs=P("row", "col"), check_vma=False,
    )
```

```python
import functools

import jax
import jax.numpy as jnp
from jax import lax
from jax.experimental import pallas as pl
from jax.experimental.pallas import tpu as pltpu
from jax.sharding import PartitionSpec as P

ITERS = 3
CHUNKS = 12
PIECES = 3
SLABS = 3
LEFT_1, ABOVE_1, LEFT_2, ABOVE_2 = range(4)
MESH = pl.DeviceIdType.MESH


def parts(x):
    high = x.astype(jnp.bfloat16)
    low = (x - high.astype(jnp.float32)).astype(jnp.bfloat16)
    return high, low


def as_left(x):
    high, low = parts(x)
    return jnp.concatenate([high, high, low], axis=1)


def as_right(x):
    high, low = parts(x)
    return jnp.concatenate([high, low, high], axis=0)


def product(left_side, right_side):
    return jnp.dot(left_side, right_side, preferred_element_type=jnp.float32)


def kernel(rows, cols, rhs_in, a_in, b_in, u_in, v_in, out_ref, rhs_ref, a_ref, b_ref, u_ref,
           v_ref, held, lefts, rights, total, send_sem, recv_sem, load_sem):
    i, j = lax.axis_index("row"), lax.axis_index("col")
    nb = rhs_ref.shape[0]
    size = nb // CHUNKS
    front = rows - 1
    s = i + j
    on_first, on_second, on_trail = s == front, s == front + 1, s >= front + 2
    place = {"row": (i, rows), "col": (j, cols)}
    on_front = on_first | on_second

    def load(which, act):
        origin, target = (
            (u_in, u_ref), (v_in, v_ref), (rhs_in, rhs_ref), (a_in, a_ref), (b_in, b_ref)
        )[which]
        depth = origin.shape[0] // PIECES
        for piece in range(PIECES):
            span = pl.ds(piece * depth, depth)
            act(pltpu.make_async_copy(
                origin.at[span], target.at[span], load_sem.at[which, piece]))

    start = lambda copy: copy.start()
    wait = lambda copy: copy.wait()

    @pl.when(on_front)
    def _():
        load(0, start)
        load(1, start)

    load(2, start)

    @pl.when(s > front)
    def _():
        load(3, start)
        load(4, start)

    barrier = pltpu.get_barrier_semaphore()
    count = jnp.int32(0)
    for axis, (k, n) in place.items():
        for by in (-2, -1, 1, 2):
            there = (k + by >= 0) & (k + by < n)
            count = count + there.astype(jnp.int32)

            @pl.when(there)
            def _():
                pl.semaphore_signal(barrier, inc=1, device_id={axis: k + by}, device_id_type=MESH)

    def flow_axis(flow):
        return "col" if flow in (LEFT_1, LEFT_2) else "row"

    def hops(flow):
        axis = flow_axis(flow)
        k, n = place[axis]
        even = lax.rem(k, 2) == 0
        source = front + (flow in (LEFT_2, ABOVE_2)) - (i if axis == "col" else j)
        if axis == "col":
            return (1, (k + 1 < n) & (even | (k == source))), (2, (k + 2 < n) & even)
        odd_source = (source & 1) == 1
        return (
            (1, (k + 1 < n) & even & (k != source + 1)),
            (2, (k + 2 < n) & (even | (k == source))),
            (-1, odd_source & (k == source + 2)),
        )

    def forwards(flow):
        return functools.reduce(jnp.logical_or, [goes for _, goes in hops(flow)])

    def each_send(flow, holds, source, c, act):
        axis = flow_axis(flow)
        k, _ = place[axis]
        span = pl.ds(pl.multiple_of(c * size, size), size)
        for slot, (by, goes) in enumerate(hops(flow)):
            @pl.when(holds & goes)
            def _():
                act(pltpu.make_async_remote_copy(
                    src_ref=source.at[span], dst_ref=held.at[flow, span],
                    send_sem=send_sem.at[flow, slot, c], recv_sem=recv_sem.at[flow, c],
                    device_id={axis: k + by}, device_id_type=MESH))

    def receive(flow, c):
        span = pl.ds(pl.multiple_of(c * size, size), size)
        pltpu.make_async_remote_copy(
            src_ref=held.at[flow, span], dst_ref=held.at[flow, span],
            send_sem=send_sem.at[flow, 0, c], recv_sem=recv_sem.at[flow, c],
            device_id={"row": i}, device_id_type=MESH).wait_recv()

    wait_send = lambda copy: copy.wait_send()
    yes = jnp.bool_(True)

    def relay(flows):
        def step(c, carry):
            for flow, valid in flows:
                @pl.when(valid & forwards(flow))
                def _():
                    receive(flow, c)
                    each_send(flow, yes, held.at[flow], c, start)
            return carry
        lax.fori_loop(0, CHUNKS, step, 0)

    def collect(flow, valid):
        @pl.when(valid & jnp.logical_not(forwards(flow)))
        def _():
            def step(c, carry):
                receive(flow, c)
                return carry
            lax.fori_loop(0, CHUNKS, step, 0)

    above_1 = j <= front
    above_2 = j <= front + 1

    @pl.when(on_front)
    def _():
        for which, source, sides, make in (
            (0, u_ref, lefts, as_left), (1, v_ref, rights, as_right)
        ):
            load(which, wait)
            power = source[...]
            sides[0] = make(power)
            for step in range(1, ITERS):
                if make is as_left:
                    power = product(sides[step - 1], as_right(power))
                else:
                    power = product(as_left(power), sides[step - 1])
                sides[step] = make(power)

    load(2, wait)

    @pl.when(on_front)
    def _():
        total[...] = rhs_ref[...]

    @pl.when(s < front)
    def _():
        out_ref[...] = rhs_ref[...]

    @pl.when(s > front)
    def _():
        load(3, wait)
        load(4, wait)

    @pl.when(on_second)
    def _():
        lefts[ITERS] = as_left(a_ref[:, :nb])
        rights[ITERS] = as_right(b_ref[:nb, :])

    @pl.when(on_trail)
    def _():
        for step in range(2):
            lefts[step] = as_left(a_ref[:, step * nb:(step + 1) * nb])
            rights[step] = as_right(b_ref[step * nb:(step + 1) * nb, :])

    pl.semaphore_wait(barrier, count)

    @pl.when(s > front)
    def _():
        relay(((ABOVE_1, above_1),))
        relay(((LEFT_1, yes),))
        collect(LEFT_1, yes)
        collect(ABOVE_1, above_1)

    @pl.when(on_second)
    def _():
        total[...] -= product(as_left(held[LEFT_1]), rights[ITERS])

        @pl.when(above_1)
        def _():
            total[...] -= product(lefts[ITERS], as_right(held[ABOVE_1]))

    @pl.when(on_front)
    def _():
        block = total[...]
        scaled = block + product(lefts[0], as_right(block))
        iterate = 0.5 * (scaled + product(as_left(scaled), rights[0]))
        for step in range(ITERS - 1):
            middle = product(as_left(iterate), rights[step])
            iterate = iterate + product(lefts[step], as_right(middle))
        total[...] = iterate
        rights[ITERS] = as_right(product(as_left(iterate), rights[ITERS - 1]))

        def send(c, carry):
            each_send(ABOVE_1, on_first, out_ref, c, start)
            each_send(LEFT_1, on_first, out_ref, c, start)
            each_send(LEFT_2, on_second, out_ref, c, start)
            each_send(ABOVE_2, on_second, out_ref, c, start)
            return carry

        depth = nb // SLABS
        for slab in range(SLABS):
            span = pl.ds(slab * depth, depth)
            out_ref[span] = total[span] + product(lefts[ITERS - 1, span], rights[ITERS])
            each = CHUNKS // SLABS
            lax.fori_loop(slab * each, (slab + 1) * each, send, 0)

    @pl.when(on_trail)
    def _():
        total[...] = product(as_left(held[LEFT_1]), rights[0])

        @pl.when(above_1)
        def _():
            total[...] += product(lefts[0], as_right(held[ABOVE_1]))

        relay(((LEFT_2, yes), (ABOVE_2, above_2)))
        collect(LEFT_2, yes)

        total[...] += product(as_left(held[LEFT_2]), rights[1])
        collect(ABOVE_2, above_2)

        @pl.when(above_2)
        def _():
            total[...] += product(lefts[1], as_right(held[ABOVE_2]))

        out_ref[...] = rhs_ref[...] - total[...]

    def finish(c, carry):
        each_send(LEFT_1, s >= front, held.at[LEFT_1], c, wait_send)
        each_send(ABOVE_1, (s >= front) & above_1, held.at[ABOVE_1], c, wait_send)
        each_send(LEFT_2, s >= front + 1, held.at[LEFT_2], c, wait_send)
        each_send(ABOVE_2, (s >= front + 1) & above_2, held.at[ABOVE_2], c, wait_send)
        return carry
    lax.fori_loop(0, CHUNKS, finish, 0)


def body(rows, cols, rhs, a_pair, b_pair, u_cay, v_cay):
    nb = rhs.shape[0]
    return pl.pallas_call(
        functools.partial(kernel, rows, cols),
        out_shape=jax.ShapeDtypeStruct(rhs.shape, jnp.float32),
        in_specs=[pl.BlockSpec(memory_space=pltpu.HBM)] * 5,
        out_specs=pl.BlockSpec(memory_space=pltpu.VMEM),
        scratch_shapes=[
            pltpu.VMEM(rhs.shape, jnp.float32),
            pltpu.VMEM(a_pair.shape, jnp.float32),
            pltpu.VMEM(b_pair.shape, jnp.float32),
            pltpu.VMEM(u_cay.shape, jnp.float32),
            pltpu.VMEM(v_cay.shape, jnp.float32),
            pltpu.VMEM((4, nb, nb), jnp.float32),
            pltpu.VMEM((ITERS + 1, nb, 3 * nb), jnp.bfloat16),
            pltpu.VMEM((ITERS + 1, 3 * nb, nb), jnp.bfloat16),
            pltpu.VMEM((nb, nb), jnp.float32),
            pltpu.SemaphoreType.DMA((4, 3, CHUNKS)),
            pltpu.SemaphoreType.DMA((4, CHUNKS)),
            pltpu.SemaphoreType.DMA((5, PIECES)),
        ],
        compiler_params=pltpu.CompilerParams(
            collective_id=0, has_side_effects=True, vmem_limit_bytes=62 * 2**20
        ),
    )(rhs, a_pair, b_pair, u_cay, v_cay)


def solution(mesh):
    placed = (P("row", "col"), P("row", "col"), P("row", "col"), P("row", None), P(None, "col"))
    return jax.shard_map(
        functools.partial(body, mesh.shape["row"], mesh.shape["col"]),
        mesh=mesh, in_specs=placed, out_specs=P("row", "col"), check_vma=False,
    )
```

```python
import functools

import jax
import jax.numpy as jnp
from jax import lax
from jax.experimental import pallas as pl
from jax.experimental.pallas import tpu as pltpu
from jax.sharding import PartitionSpec as P

ITERS = 3
CHUNKS = 6
PIECES = 3
SLABS = 3
LEFT_1, ABOVE_1, LEFT_2, ABOVE_2 = range(4)
MESH = pl.DeviceIdType.MESH


def parts(x):
    high = x.astype(jnp.bfloat16)
    low = (x - high.astype(jnp.float32)).astype(jnp.bfloat16)
    return high, low


def as_left(x):
    high, low = parts(x)
    return jnp.concatenate([high, high, low], axis=1)


def as_right(x):
    high, low = parts(x)
    return jnp.concatenate([high, low, high], axis=0)


def product(left_side, right_side):
    return jnp.dot(left_side, right_side, preferred_element_type=jnp.float32)


def kernel(rows, cols, rhs_in, a_in, b_in, u_in, v_in, out_ref, rhs_ref, a_ref, b_ref, u_ref,
           v_ref, held, lefts, rights, total, send_sem, recv_sem, load_sem):
    i, j = lax.axis_index("row"), lax.axis_index("col")
    nb = rhs_ref.shape[0]
    size = nb // CHUNKS
    front = rows - 1
    s = i + j
    on_first, on_second, on_trail = s == front, s == front + 1, s >= front + 2
    place = {"row": (i, rows), "col": (j, cols)}
    on_front = on_first | on_second

    def load(which, act):
        origin, target = (
            (u_in, u_ref), (v_in, v_ref), (rhs_in, rhs_ref), (a_in, a_ref), (b_in, b_ref)
        )[which]
        depth = origin.shape[0] // PIECES
        for piece in range(PIECES):
            span = pl.ds(piece * depth, depth)
            act(pltpu.make_async_copy(
                origin.at[span], target.at[span], load_sem.at[which, piece]))

    start = lambda copy: copy.start()
    wait = lambda copy: copy.wait()

    @pl.when(on_front)
    def _():
        load(0, start)
        load(1, start)

    load(2, start)

    @pl.when(s > front)
    def _():
        load(3, start)
        load(4, start)

    barrier = pltpu.get_barrier_semaphore()
    count = jnp.int32(0)
    for axis, (k, n) in place.items():
        for by in (-2, -1, 1, 2):
            there = (k + by >= 0) & (k + by < n)
            count = count + there.astype(jnp.int32)

            @pl.when(there)
            def _():
                pl.semaphore_signal(barrier, inc=1, device_id={axis: k + by}, device_id_type=MESH)

    def flow_axis(flow):
        return "col" if flow in (LEFT_1, LEFT_2) else "row"

    def hops(flow):
        axis = flow_axis(flow)
        k, n = place[axis]
        even = lax.rem(k, 2) == 0
        source = front + (flow in (LEFT_2, ABOVE_2)) - (i if axis == "col" else j)
        if axis == "col":
            return (1, (k + 1 < n) & (even | (k == source))), (2, (k + 2 < n) & even)
        odd_source = (source & 1) == 1
        return (
            (1, (k + 1 < n) & even & (k != source + 1)),
            (2, (k + 2 < n) & (even | (k == source))),
            (-1, odd_source & (k == source + 2)),
        )

    def forwards(flow):
        return functools.reduce(jnp.logical_or, [goes for _, goes in hops(flow)])

    def each_send(flow, holds, source, c, act):
        axis = flow_axis(flow)
        k, _ = place[axis]
        span = pl.ds(pl.multiple_of(c * size, size), size)
        for slot, (by, goes) in enumerate(hops(flow)):
            @pl.when(holds & goes)
            def _():
                act(pltpu.make_async_remote_copy(
                    src_ref=source.at[span], dst_ref=held.at[flow, span],
                    send_sem=send_sem.at[flow, slot, c], recv_sem=recv_sem.at[flow, c],
                    device_id={axis: k + by}, device_id_type=MESH))

    def receive(flow, c):
        span = pl.ds(pl.multiple_of(c * size, size), size)
        pltpu.make_async_remote_copy(
            src_ref=held.at[flow, span], dst_ref=held.at[flow, span],
            send_sem=send_sem.at[flow, 0, c], recv_sem=recv_sem.at[flow, c],
            device_id={"row": i}, device_id_type=MESH).wait_recv()

    wait_send = lambda copy: copy.wait_send()
    yes = jnp.bool_(True)

    def relay(flows):
        def step(c, carry):
            for flow, valid in flows:
                @pl.when(valid & forwards(flow))
                def _():
                    receive(flow, c)
                    each_send(flow, yes, held.at[flow], c, start)
            return carry
        lax.fori_loop(0, CHUNKS, step, 0)

    def collect(flow, valid, first=0, last=CHUNKS):
        @pl.when(valid & jnp.logical_not(forwards(flow)))
        def _():
            def step(c, carry):
                receive(flow, c)
                return carry
            lax.fori_loop(first, last, step, 0)

    above_1 = j <= front
    above_2 = j <= front + 1

    @pl.when(on_front)
    def _():
        for which, source, sides, make in (
            (0, u_ref, lefts, as_left), (1, v_ref, rights, as_right)
        ):
            load(which, wait)
            power = source[...]
            sides[0] = make(power)
            for step in range(1, ITERS):
                if make is as_left:
                    power = product(sides[step - 1], as_right(power))
                else:
                    power = product(as_left(power), sides[step - 1])
                sides[step] = make(power)

    load(2, wait)

    @pl.when(on_front)
    def _():
        total[...] = rhs_ref[...]

    @pl.when(s < front)
    def _():
        out_ref[...] = rhs_ref[...]

    @pl.when(s > front)
    def _():
        load(3, wait)
        load(4, wait)

    @pl.when(on_second)
    def _():
        lefts[ITERS] = as_left(a_ref[:, :nb])
        rights[ITERS] = as_right(b_ref[:nb, :])

    @pl.when(on_trail)
    def _():
        for step in range(2):
            lefts[step] = as_left(a_ref[:, step * nb:(step + 1) * nb])
            rights[step] = as_right(b_ref[step * nb:(step + 1) * nb, :])

    pl.semaphore_wait(barrier, count)

    @pl.when(s > front)
    def _():
        relay(((ABOVE_1, above_1),))
        relay(((LEFT_1, yes),))
        collect(LEFT_1, yes)

    @pl.when(on_second)
    def _():
        total[...] -= product(as_left(held[LEFT_1]), rights[ITERS])

    @pl.when(s > front)
    def _():
        collect(ABOVE_1, above_1)

    @pl.when(on_second)
    def _():

        @pl.when(above_1)
        def _():
            total[...] -= product(lefts[ITERS], as_right(held[ABOVE_1]))

    @pl.when(on_front)
    def _():
        block = total[...]
        scaled = block + product(lefts[0], as_right(block))
        iterate = 0.5 * (scaled + product(as_left(scaled), rights[0]))
        for step in range(ITERS - 1):
            middle = product(as_left(iterate), rights[step])
            iterate = iterate + product(lefts[step], as_right(middle))
        total[...] = iterate
        rights[ITERS] = as_right(product(as_left(iterate), rights[ITERS - 1]))

        def send(c, carry):
            each_send(ABOVE_1, on_first, out_ref, c, start)
            each_send(LEFT_1, on_first, out_ref, c, start)
            each_send(LEFT_2, on_second, out_ref, c, start)
            each_send(ABOVE_2, on_second, out_ref, c, start)
            return carry

        depth = nb // SLABS
        for slab in range(SLABS):
            span = pl.ds(slab * depth, depth)
            out_ref[span] = total[span] + product(lefts[ITERS - 1, span], rights[ITERS])
            each = CHUNKS // SLABS
            lax.fori_loop(slab * each, (slab + 1) * each, send, 0)

    @pl.when(on_trail)
    def _():
        total[...] = product(as_left(held[LEFT_1]), rights[0])

        @pl.when(above_1)
        def _():
            total[...] += product(lefts[0], as_right(held[ABOVE_1]))

        relay(((LEFT_2, yes), (ABOVE_2, above_2)))
        each, depth = CHUNKS // SLABS, nb // SLABS
        for slab in range(SLABS):
            collect(LEFT_2, yes, slab * each, (slab + 1) * each)
            span = pl.ds(slab * depth, depth)
            total[span] += product(as_left(held[LEFT_2, span]), rights[1])

        collect(ABOVE_2, above_2)

        @pl.when(above_2)
        def _():
            total[...] += product(lefts[1], as_right(held[ABOVE_2]))

        out_ref[...] = rhs_ref[...] - total[...]

    def finish(c, carry):
        each_send(LEFT_1, s >= front, held.at[LEFT_1], c, wait_send)
        each_send(ABOVE_1, (s >= front) & above_1, held.at[ABOVE_1], c, wait_send)
        each_send(LEFT_2, s >= front + 1, held.at[LEFT_2], c, wait_send)
        each_send(ABOVE_2, (s >= front + 1) & above_2, held.at[ABOVE_2], c, wait_send)
        return carry
    lax.fori_loop(0, CHUNKS, finish, 0)


def body(rows, cols, rhs, a_pair, b_pair, u_cay, v_cay):
    nb = rhs.shape[0]
    return pl.pallas_call(
        functools.partial(kernel, rows, cols),
        out_shape=jax.ShapeDtypeStruct(rhs.shape, jnp.float32),
        in_specs=[pl.BlockSpec(memory_space=pltpu.HBM)] * 5,
        out_specs=pl.BlockSpec(memory_space=pltpu.VMEM),
        scratch_shapes=[
            pltpu.VMEM(rhs.shape, jnp.float32),
            pltpu.VMEM(a_pair.shape, jnp.float32),
            pltpu.VMEM(b_pair.shape, jnp.float32),
            pltpu.VMEM(u_cay.shape, jnp.float32),
            pltpu.VMEM(v_cay.shape, jnp.float32),
            pltpu.VMEM((4, nb, nb), jnp.float32),
            pltpu.VMEM((ITERS + 1, nb, 3 * nb), jnp.bfloat16),
            pltpu.VMEM((ITERS + 1, 3 * nb, nb), jnp.bfloat16),
            pltpu.VMEM((nb, nb), jnp.float32),
            pltpu.SemaphoreType.DMA((4, 3, CHUNKS)),
            pltpu.SemaphoreType.DMA((4, CHUNKS)),
            pltpu.SemaphoreType.DMA((5, PIECES)),
        ],
        compiler_params=pltpu.CompilerParams(
            collective_id=0, has_side_effects=True, vmem_limit_bytes=62 * 2**20
        ),
    )(rhs, a_pair, b_pair, u_cay, v_cay)


def solution(mesh):
    placed = (P("row", "col"), P("row", "col"), P("row", "col"), P("row", None), P(None, "col"))
    return jax.shard_map(
        functools.partial(body, mesh.shape["row"], mesh.shape["col"]),
        mesh=mesh, in_specs=placed, out_specs=P("row", "col"), check_vma=False,
    )
```
